256 devices in a mesh: layer: 4 (over x), feat: 64 (over z, y, core).
Axes of the slice: x: 4, y: 4, z: 8, core: 2. Of those that a mesh axis runs over, the one named last changes fastest.
Arguments:
- resid: bfloat16 [512, 4, 2048], P(('layer', 'feat')), may hold values from -6 to 6
- target: bfloat16 [512, 4, 2048], P(('layer', 'feat')), may hold values from -6 to 6
- enc_weight: bfloat16 [4, 2048, 16384], P('layer', None, 'feat'), may hold values from -0.125 to 0.125
- enc_bias: float32 [4, 16384], P('layer', 'feat'), may hold values from -3 to 3
- dec_weight: bfloat16 [4, 4, 16384, 2048], P('layer', None, 'feat'), may hold values from -5 to 5
- dec_bias: float32 [4, 2048], P('layer'), may hold values from -3 to 3
Outputs:
- dec_grad: bfloat16 [4, 4, 16384, 2048], P('layer', None, 'feat')
The draws below stay inside these ranges and needn't reach their ends.
All inputs are finite; a program needn't handle non-finite values.
Results may differ from the reference program's by a relative error of at most 0.0023.
Values may be sent and summed in bfloat16 or wider, within the bound.
No kernel may reach another device: no remote copies, remote signals or barrier semaphores. Data moves between devices by JAX's collectives and lax.ppermute only.
A program may use at most 128 MiB of HBM per device.

```python
import math
import jax
import jax.numpy as jnp

D = 2048
FEAT = 16384
TOKENS = 512
LAYERS = 4
FDEV = 256


def draw_dec_weight(key, part):
    key = jax.random.fold_in(key, 7)
    base = jax.random.truncated_normal(key, -4.0, 4.0, (LAYERS, LAYERS, FEAT, D), jnp.float32)
    block = jnp.arange(FEAT) // FDEV
    column = jnp.arange(D) % (FEAT // FDEV)
    heavy = jnp.where(block[:, None] == column[None, :], 8.0, 1.0)
    values = base * heavy[None, None, :, :] / math.sqrt(FEAT)
    return jnp.clip(values, -5.0, 5.0).astype(jnp.bfloat16)


def levels(own_key, dims, split, least, top_value):
    level, own = 1.0, jax.random.fold_in(own_key, 6)
    for dim, parts in split:
        draws = jnp.exp(jax.random.uniform(jax.random.fold_in(own, dim), (parts,), jnp.float32, least / len(split), top_value / len(split)))
        level = level * jnp.repeat(draws, dims[dim] // parts).reshape([-1 if axis == dim else 1 for axis in range(len(dims))])
    return level


def bell_draw(stream_key, dims, deviation, most, shards=(), dtype=jnp.bfloat16):
    result = deviation * jax.random.normal(stream_key, dims, jnp.float32)
    if shards:
        result = result * levels(stream_key, dims, shards, -0.22, 0.18)
    return jnp.clip(result, -most, most).astype(dtype)


def setup_inputs(seed: int = 0) -> dict:
    key_list = jax.random.split(jax.random.key(seed), 7)
    resid = bell_draw(key_list[0], (TOKENS, LAYERS, D), 1.0, 6.0, ((0, 256),))
    target = bell_draw(key_list[1], (TOKENS, LAYERS, D), 1.0, 6.0, ((0, 256),))
    enc_weight = bell_draw(key_list[2], (LAYERS, D, FEAT), D ** -0.5, 0.125, ((0, 4), (2, 64)))
    enc_bias = bell_draw(key_list[3], (LAYERS, FEAT), 0.5, 3.0, ((0, 4), (1, 64)), jnp.float32)
    dec_weight = draw_dec_weight(jax.random.fold_in(key_list[6], 71), 0)
    dec_bias = bell_draw(key_list[5], (LAYERS, D), 0.5, 3.0, ((0, 4),), jnp.float32)
    return dict(resid=resid, target=target, enc_weight=enc_weight, enc_bias=enc_bias, dec_weight=dec_weight, dec_bias=dec_bias)


def reference(resid, target, enc_weight, enc_bias, dec_weight, dec_bias):
    factor = 1.0 / math.sqrt(TOKENS)
    activity = []
    for source in range(LAYERS):
        preact = jnp.dot(resid[:, source, :], enc_weight[source], preferred_element_type=jnp.float32) + enc_bias[source][None, :]
        activity.append(jax.nn.relu(preact).astype(jnp.bfloat16))
    cotangent = []
    for sink in range(LAYERS):
        recon = jnp.zeros((TOKENS, D), jnp.float32) + dec_bias[sink][None, :]
        for source in range(sink + 1):
            recon = recon + jnp.dot(activity[source], dec_weight[source, sink], preferred_element_type=jnp.float32)
        misfit = recon - target[:, sink, :].astype(jnp.float32)
        cotangent.append((misfit * factor).astype(jnp.bfloat16))
    rows = []
    for source in range(LAYERS):
        blocks = []
        for sink in range(LAYERS):
            if sink >= source:
                blocks.append(jnp.dot(activity[source].T, cotangent[sink], preferred_element_type=jnp.float32).astype(jnp.bfloat16))
            else:
                blocks.append(jnp.zeros((FEAT, D), jnp.bfloat16))
        rows.append(jnp.stack(blocks))
    return jnp.stack(rows)
```

```python
import functools
import math

import jax
import jax.numpy as jnp
from jax import lax
from jax.experimental import pallas as pl
from jax.experimental.pallas import tpu as pltpu
from jax.sharding import Mesh
from jax.sharding import PartitionSpec as P

BF = jnp.bfloat16
F32 = jnp.float32
NX, NZ, NY, NC = 4, 8, 4, 2
XZ = NX * NZ
VMEM_LIMIT = 48 * 1024 * 1024


def shift(value, axis, step):
    size = lax.axis_size(axis)
    return lax.ppermute(value, axis, [(i, (i + step) % size) for i in range(size)])


def encoder_kernel(x0, x1, x2, x3, others, weight, bias, place, out, rows):
    chunk = x0.shape[0]
    for i, ref in enumerate((x0, x1, x2, x3)):
        rows[i * chunk:(i + 1) * chunk, :] = ref[...]
        rows[(NY + i) * chunk:(NY + i + 1) * chunk, :] = others[i]
    preact = jnp.dot(rows[...], weight[...], preferred_element_type=F32) + bias[...]
    activity = jnp.maximum(preact, 0.0).astype(BF)
    out[...] = jnp.dot(place[...], activity, preferred_element_type=F32).astype(BF)


def encode(own, others, weight, bias, place):
    tokens = place.shape[0]
    return pl.pallas_call(
        encoder_kernel,
        out_shape=jax.ShapeDtypeStruct((tokens, weight.shape[1]), BF),
        scratch_shapes=[pltpu.VMEM((tokens, weight.shape[0]), BF)],
        compiler_params=pltpu.CompilerParams(vmem_limit_bytes=VMEM_LIMIT),
        name="encode",
    )(*own, others, weight, bias, place)


def decoder_kernel(layer, r0, r1, r2, r3, a0, a1, a2, a3, others, bias, out):
    sink = pl.program_id(0)

    @pl.when(sink >= layer[0])
    def _():
        total = jnp.zeros(a0.shape[:1] + r0.shape[3:], F32)
        for i, (r, a) in enumerate(((r0, a0), (r1, a1), (r2, a2), (r3, a3))):
            total += jnp.dot(a[...], r[0, 0], preferred_element_type=F32)
            total += jnp.dot(others[i], r[1, 0], preferred_element_type=F32)
        total += bias[0]
        out[...] = total.astype(BF).reshape(out.shape)

    @pl.when(sink < layer[0])
    def _():
        out[...] = jnp.zeros(out.shape, BF)


def decode(layer, weights, own, others, bias):
    sinks, feats, cols = weights[0].shape[1:]
    tokens = own[0].shape[0]
    part = tokens // XZ
    return pl.pallas_call(
        decoder_kernel,
        grid_spec=pltpu.PrefetchScalarGridSpec(
            num_scalar_prefetch=1,
            grid=(sinks,),
            in_specs=[pl.BlockSpec((2, 1, feats, cols), lambda m, _: (0, m, 0, 0))] * NY
            + [pl.BlockSpec((tokens, feats), lambda m, _: (0, 0))] * NY
            + [pl.BlockSpec((NY, tokens, feats), lambda m, _: (0, 0, 0))]
            + [pl.BlockSpec((1, 1, cols), lambda m, _: (m, 0, 0))],
            out_specs=pl.BlockSpec((XZ, 1, part, cols), lambda m, _: (0, m, 0, 0)),
        ),
        out_shape=jax.ShapeDtypeStruct((XZ, sinks, part, cols), BF),
        compiler_params=pltpu.CompilerParams(vmem_limit_bytes=VMEM_LIMIT),
        name="decode",
    )(layer, *weights, *own, others, bias)


def gradient_kernel(place, c0, c1, c2, c3, others, activity, out):
    sink = pl.program_id(0)
    layer, y, core = place[0], place[1], place[2]
    cols = c0.shape[3]

    @pl.when(sink >= layer)
    def _():
        for i, c in enumerate((c0, c1, c2, c3)):
            quarter = lax.rem(y + NY - i, NY)
            for half, block in ((core, c[:, 0]), (1 - core, others[i, :, 0])):
                start = pl.multiple_of((half * NY + quarter) * cols, cols)
                grad = jnp.dot(activity[...], block.reshape(-1, cols), preferred_element_type=F32)
                out[0, :, pl.ds(start, cols)] = grad.astype(BF)

    @pl.when(sink < layer)
    def _():
        out[...] = jnp.zeros(out.shape, BF)


def gradient(place, own, others, activity):
    slots, sinks, part, cols = own[0].shape
    feats, tokens = activity.shape
    return pl.pallas_call(
        gradient_kernel,
        grid_spec=pltpu.PrefetchScalarGridSpec(
            num_scalar_prefetch=1,
            grid=(sinks,),
            in_specs=[pl.BlockSpec((slots, 1, part, cols), lambda m, _: (0, m, 0, 0))] * NY
            + [pl.BlockSpec((NY, slots, 1, part, cols), lambda m, _: (0, 0, m, 0, 0))]
            + [pl.BlockSpec((feats, tokens), lambda m, _: (0, 0))],
            out_specs=pl.BlockSpec((1, feats, NY * NC * cols), lambda m, _: (m, 0, 0)),
        ),
        out_shape=jax.ShapeDtypeStruct((sinks, feats, NY * NC * cols), BF),
        compiler_params=pltpu.CompilerParams(vmem_limit_bytes=VMEM_LIMIT),
        name="gradient",
    )(place, *own, others, activity)


def body(resid, target, enc_weight, enc_bias, dec_weight, dec_bias):
    x, z, y, core = (lax.axis_index(a) for a in ("x", "z", "y", "c"))
    mine, layers, width = resid.shape
    tokens = mine * XZ * NY * NC
    half, cols = width // NC, width // (NC * NY)
    factor = 1.0 / math.sqrt(tokens)
    weight = dec_weight[0]
    feats = weight.shape[1]

    keep = lax.dynamic_slice_in_dim(weight, core * half, half, axis=2)
    give = lax.dynamic_slice_in_dim(weight, (1 - core) * half, half, axis=2)
    both = jnp.stack([keep, shift(give, "c", 1)])
    weights = []
    for step in range(NY):
        piece = lax.dynamic_slice_in_dim(both, lax.rem(y + step, NY) * cols, cols, axis=3)
        weights.append(piece if step == 0 else shift(piece, "y", step))

    rows = jnp.broadcast_to(resid.transpose(1, 0, 2)[:, None], (layers, NZ, mine, width))
    rows = lax.all_to_all(rows.reshape(XZ * mine, width), ("x", "z"), 0, 0, tiled=True)
    own = [rows] + [shift(rows, "y", step) for step in range(1, NY)]
    others = shift(jnp.stack(own), "c", 1)
    r = jnp.arange(tokens)
    r_half, r_step, r_slot, r_i = r // (tokens // 2), r // (tokens // 8) % NY, r // mine % XZ, r % mine
    r_core = jnp.where(r_half == 0, core, 1 - core)
    token = ((r_slot * NY + (y + NY - r_step) % NY) * NC + r_core) * mine + r_i
    place = (jnp.arange(tokens)[:, None] == token[None, :]).astype(BF)
    activity = encode(own, others, enc_weight[0], enc_bias, place)

    acts = [activity] + [shift(activity, "y", step) for step in range(1, NY)]
    act_others = shift(jnp.stack(acts), "c", 1)
    column = core * half + y * cols
    bias = lax.dynamic_slice_in_dim(dec_bias[0], column, cols)
    bias = jnp.where(((jnp.arange(layers) == x) & (z == 0))[:, None, None], bias[None, None, :], 0.0)
    parts = decode(x.reshape(1), weights, acts, act_others, bias)

    wanted = target.reshape(mine, layers, NC, NY, cols).transpose(3, 2, 1, 0, 4)
    wanted = lax.all_to_all(wanted.reshape(NY * NC, layers, mine, cols), ("y", "c"), 0, 0, tiled=True)
    wanted = wanted.transpose(1, 0, 2, 3).reshape(layers, NY * NC * mine, cols)
    got = lax.all_to_all(parts, ("x", "z"), 0, 0, tiled=True)
    misfit = jnp.sum(got.astype(F32), axis=0) - wanted.astype(F32)
    cotangent = (misfit * factor).astype(BF)

    copies = jnp.broadcast_to(cotangent[None], (XZ,) + cotangent.shape)
    block = lax.all_to_all(copies, ("x", "z"), 0, 0, tiled=True)
    blocks = [block] + [shift(block, "y", step) for step in range(1, NY)]
    block_others = shift(jnp.stack(blocks), "c", 1)
    grads = gradient(jnp.stack([x, y, core]), blocks, block_others, activity.T)
    return grads[None]


def solution(mesh):
    fine = Mesh(mesh.devices.reshape(NX, NZ, NY, NC), ("x", "z", "y", "c"))
    feat = ("z", "y", "c")
    return jax.shard_map(
        body,
        mesh=fine,
        in_specs=(
            P(("x",) + feat, None, None),
            P(("x",) + feat, None, None),
            P("x", None, feat),
            P("x", feat),
            P("x", None, feat, None),
            P("x", None),
        ),
        out_specs=P("x", None, feat, None),
        check_vma=False,
    )
```

```python
import functools
import math

import jax
import jax.numpy as jnp
from jax import lax
from jax.experimental import pallas as pl
from jax.experimental.pallas import tpu as pltpu
from jax.sharding import Mesh
from jax.sharding import PartitionSpec as P

BF = jnp.bfloat16
F32 = jnp.float32
NX, NZ, NY, NC = 4, 8, 4, 2
XZ = NX * NZ

ALL = ("x", "z", "y", "c")
VMEM_LIMIT = 24 * 1024 * 1024


def device(x, z, y, core):
    return ((x * NZ + z) * NY + y) * NC + core


def coordinates():
    return [(x, z, y, core) for x in range(NX) for z in range(NZ) for y in range(NY) for core in range(NC)]


def shift(value, axis, step):
    size = lax.axis_size(axis)
    return lax.ppermute(value, axis, [(i, (i + step) % size) for i in range(size)])


def ring(value, step):
    pairs = []
    for x, z, y, core in coordinates():
        there = (x, z, (y + step) % NY, core) if core == 0 else ((x + step) % NX, z, y, core)
        pairs.append((device(x, z, y, core), device(*there)))
    return lax.ppermute(value, ALL, pairs)


def trade(value):
    groups = [[device(x, z, y, 0) for x in range(NX) for z in range(NZ)] for y in range(NY)]
    groups += [[device(x, z, y, 1) for y in range(NY) for z in range(NZ)] for x in range(NX)]
    return lax.all_to_all(value, ALL, 0, 0, axis_index_groups=groups, tiled=True)


def encoder_kernel(*refs):
    pieces, (weight, bias, place, mine, give, rows) = refs[:NY * NC], refs[NY * NC:]
    chunk = pieces[0].shape[0]
    for i, ref in enumerate(pieces):
        rows[i * chunk:(i + 1) * chunk, :] = ref[...]
    preact = jnp.dot(rows[...], weight[...], preferred_element_type=F32) + bias[...]
    activity = jnp.maximum(preact, 0.0).astype(BF)
    mine[...] = jnp.dot(place[0], activity, preferred_element_type=F32).astype(BF)
    give[...] = jnp.dot(place[1], activity, preferred_element_type=F32).astype(BF)


def encode(pieces, weight, bias, place):
    tokens = place.shape[1]
    result = jax.ShapeDtypeStruct((tokens, weight.shape[1]), BF)
    return pl.pallas_call(
        encoder_kernel,
        out_shape=(result, result),
        scratch_shapes=[pltpu.VMEM((tokens, weight.shape[0]), BF)],
        compiler_params=pltpu.CompilerParams(vmem_limit_bytes=VMEM_LIMIT),
        cost_estimate=pl.CostEstimate(flops=8 * 10**8, bytes_accessed=4 * 10**6, transcendentals=0),
        name="encode",
    )(*pieces, weight, bias, place)


def decoder_kernel(where, a0, a1, a2, a3, w0, w1, w2, w3, bias, out, total):
    feats = a0.shape[2]
    x, z, y, core = (where[i] for i in range(4))
    adds_bias = (z == 0) & (((core == 0) & (x == y)) | ((core == 1) & (y == 0)))
    total[...] = jnp.broadcast_to(jnp.where(adds_bias, bias[...], 0.0), total.shape)
    for i, (a, w) in enumerate(((a0, w0), (a1, w1), (a2, w2), (a3, w3))):

        @pl.when(((core == 0) & (y >= x)) | ((core == 1) & (x >= i)))
        def _():
            total[...] += jnp.dot(a[0], w[:feats, :], preferred_element_type=F32) + jnp.dot(
                a[1], w[feats:2 * feats, :], preferred_element_type=F32
            )

    out[...] = total[...].astype(BF).reshape(out.shape)


def decode(where, acts, weights, bias):
    cores, tokens, feats = acts[0].shape
    rows, width = weights[0].shape
    part, cols = tokens // XZ, 256
    blocks = width // cols
    return pl.pallas_call(
        decoder_kernel,
        grid_spec=pltpu.PrefetchScalarGridSpec(
            num_scalar_prefetch=1,
            grid=(blocks,),
            in_specs=[pl.BlockSpec((cores, tokens, feats), lambda n, _: (0, 0, 0))] * NY
            + [pl.BlockSpec((rows, cols), lambda n, _: (0, n))] * NY
            + [pl.BlockSpec((1, cols), lambda n, where: (0, where[3] * blocks + n))],
            out_specs=pl.BlockSpec((XZ, part, cols), lambda n, _: (0, 0, n)),
            scratch_shapes=[pltpu.VMEM((tokens, cols), F32)],
        ),
        out_shape=jax.ShapeDtypeStruct((XZ, part, width), BF),
        compiler_params=pltpu.CompilerParams(vmem_limit_bytes=VMEM_LIMIT),
        cost_estimate=pl.CostEstimate(flops=22 * 10**8, bytes_accessed=8 * 10**6, transcendentals=0),
        name="decode",
    )(where, *acts, *weights, bias)


def sinks_at(where, step):
    x, y, core = where[0], where[2], where[3]
    first, second = jnp.where(core == 0, y, x), jnp.where(core == 0, x, y)
    return lax.rem(first + NY - step, NY), lax.rem(second + NY - step, NY)


def gradient_kernel(step, where, own, other, mine, give, *rest):
    out = rest[-1]
    half = pl.program_id(0)
    sinks = sinks_at(where, step)
    for i, (block, activity) in enumerate(((own, mine), (other, give))):

        @pl.when((half == i) & (sinks[i] >= where[0]))
        def _():
            rhs = block[...].reshape(-1, block.shape[2])
            out[0] = jnp.dot(activity[...], rhs, preferred_element_type=F32).astype(BF)

        @pl.when((half == i) & (sinks[i] < where[0]))
        def _():
            out[...] = jnp.zeros(out.shape, BF)


def gradient(step, where, layers, own, other, mine, give, before):
    slots, part, cols = own.shape
    feats, tokens = mine.shape
    more = [] if before is None else [before]

    def place(half, where):
        first, second = sinks_at(where, step)
        return jnp.where(half == 0, first, second), 0, jnp.where(half == 0, where[3], 1 - where[3])

    return pl.pallas_call(
        functools.partial(gradient_kernel, step),
        grid_spec=pltpu.PrefetchScalarGridSpec(
            num_scalar_prefetch=1,
            grid=(NC,),
            in_specs=[pl.BlockSpec((slots, part, cols), lambda h, _: (0, 0, 0))] * 2
            + [pl.BlockSpec((feats, tokens), lambda h, _: (0, 0))] * 2
            + [pl.BlockSpec(memory_space=pl.ANY)] * len(more),
            out_specs=pl.BlockSpec((1, feats, cols), place),
        ),
        out_shape=jax.ShapeDtypeStruct((layers, feats, NC * cols), BF),
        input_output_aliases={5: 0} if more else {},
        compiler_params=pltpu.CompilerParams(vmem_limit_bytes=VMEM_LIMIT),
        cost_estimate=pl.CostEstimate(flops=55 * 10**7, bytes_accessed=4 * 10**6, transcendentals=0),
        name="gradient",
    )(where, own, other, mine, give, *more)


def pack_kernel(where, own, other, target, out):
    feats = own.shape[1]
    out[:feats, :] = own[0]
    out[feats:2 * feats, :] = other[0]
    out[2 * feats:, :] = target[0]


def pack(step, where, weight, other, target):
    layers, feats, half = other.shape
    extra = target.shape[1]

    def sink(where):
        return lax.rem(jnp.where(where[3] == 0, where[2], where[0]) + step, NY)

    return pl.pallas_call(
        pack_kernel,
        grid_spec=pltpu.PrefetchScalarGridSpec(
            num_scalar_prefetch=1,
            grid=(2,),
            in_specs=[
                pl.BlockSpec((1, feats, half // 2), lambda n, where: (sink(where), 0, where[3] * 2 + n)),
                pl.BlockSpec((1, feats, half // 2), lambda n, where: (sink(where), 0, n)),
                pl.BlockSpec((1, extra, half // 2), lambda n, where: (sink(where), 0, n)),
            ],
            out_specs=pl.BlockSpec((2 * feats + extra, half // 2), lambda n, where: (0, n)),
        ),
        out_shape=jax.ShapeDtypeStruct((2 * feats + extra, half), BF),
        compiler_params=pltpu.CompilerParams(vmem_limit_bytes=VMEM_LIMIT),
        cost_estimate=pl.CostEstimate(flops=0, bytes_accessed=2 * 10**6, transcendentals=0),
        name="pack",
    )(where, weight, other, target)


def body(resid, target, enc_weight, enc_bias, dec_weight, dec_bias):
    x, z, y, core = (lax.axis_index(a) for a in ALL)
    mine, layers, width = resid.shape
    tokens = mine * XZ * NY * NC
    half = width // NC
    factor = 1.0 / math.sqrt(tokens)
    feats = dec_weight.shape[2]
    sink = jnp.where(core == 0, y, x)
    where = jnp.stack([x, z, y, core])

    give = lax.dynamic_slice_in_dim(dec_weight[0], (1 - core) * half, half, axis=2)
    aims = target.transpose(1, 0, 2).reshape(layers, mine, NC, half)
    aims = jnp.where(core == 0, jnp.stack([aims[:, :, 0], aims[:, :, 1]]), jnp.stack([aims[:, :, 1], aims[:, :, 0]]))
    rows = jnp.broadcast_to(resid.transpose(1, 0, 2)[:, None], (layers, NZ, mine, width))
    rows = rows.reshape(XZ * mine, width)
    rows, give, aims, where = lax.optimization_barrier((rows, give, aims, where))
    extra = jnp.concatenate([aims[0], shift(aims[1], "c", 1), jnp.zeros((layers, 16 - 2 * mine, half), BF)], axis=1)
    give = shift(give, "c", 1)
    weights = [pack(step, where, dec_weight[0], give, extra) for step in range(NY)]
    rows = lax.all_to_all(rows, ("x", "z"), 0, 0, tiled=True)
    rows, *weights = lax.optimization_barrier((rows, *weights))
    weights = [ring(piece, step) if step else piece for step, piece in enumerate(weights)]
    pieces = [rows] + [shift(rows, "y", step) for step in range(1, NY)]
    pieces = pieces + [shift(piece, "c", 1) for piece in pieces]
    r = jnp.arange(tokens)
    r_core = jnp.where(r // (tokens // 2) == 0, core, 1 - core)
    r_y = (y + NY - r // (tokens // 8) % NY) % NY
    r_x, r_z, r_i = r // (mine * NZ) % NX, r // mine % NZ, r % mine
    order = [((a * NZ + r_z) * 4 + b) * NC * mine + r_core * mine + r_i for a, b in ((r_x, r_y), (r_y, r_x))]
    order = jnp.stack([jnp.where(core == 0, order[0], order[1]), jnp.where(core == 0, order[1], order[0])])
    place = (jnp.arange(tokens)[None, :, None] == order[:, None, :]).astype(BF)
    own, away = encode(pieces, enc_weight[0], enc_bias, place)

    act = jnp.stack([own, shift(away, "c", 1)])
    acts = [act] + [ring(act, step) for step in range(1, NY)]
    parts = decode(where, acts, weights, dec_bias)

    wanted = jnp.concatenate([w[2 * feats:2 * feats + 2 * mine] for w in weights])
    q = jnp.arange(NY * NC * mine)
    q_core = jnp.where(q // mine % NC == 0, core, 1 - core)
    q = (sink + NY - q // (NC * mine)) % NY * NC * mine + q_core * mine + q % mine
    wanted = jnp.dot((jnp.arange(q.shape[0])[:, None] == q[None, :]).astype(BF), wanted, preferred_element_type=F32)

    got = trade(parts)
    own, away = own.T, away.T
    got, own, away = lax.optimization_barrier((got, own, away))
    misfit = jnp.sum(got.astype(F32), axis=0) - wanted
    cotangent = (misfit * factor).astype(BF)
    block = trade(jnp.broadcast_to(cotangent[None], (XZ,) + cotangent.shape))

    grads = None
    blocks = [block] + [ring(block, step) for step in range(1, NY)]
    for step in (0, 1, 3, 2):
        grads = gradient(step, where, layers, blocks[step], shift(blocks[step], "c", 1), own, away, grads)
    return grads[None]


def solution(mesh):
    fine = Mesh(mesh.devices.reshape(NX, NZ, NY, NC), ("x", "z", "y", "c"))
    feat = ("z", "y", "c")
    return jax.shard_map(
        body,
        mesh=fine,
        in_specs=(
            P(("x",) + feat, None, None),
            P(("x",) + feat, None, None),
            P("x", None, feat),
            P("x", feat),
            P("x", None, feat, None),
            P("x", None),
        ),
        out_specs=P("x", None, feat, None),
        check_vma=False,
    )
```

```python
import functools
import math

import jax
import jax.numpy as jnp
from jax import lax
from jax.experimental import pallas as pl
from jax.experimental.pallas import tpu as pltpu
from jax.sharding import Mesh
from jax.sharding import PartitionSpec as P

BF = jnp.bfloat16
F32 = jnp.float32
NX, NZ, NY, NC = 4, 8, 4, 2
XZ = NX * NZ

ALL = ("x", "z", "y", "c")
VMEM_LIMIT = 24 * 1024 * 1024


def device(x, z, y, core):
    return ((x * NZ + z) * NY + y) * NC + core


def coordinates():
    return [(x, z, y, core) for x in range(NX) for z in range(NZ) for y in range(NY) for core in range(NC)]


def shift(value, axis, step):
    size = lax.axis_size(axis)
    return lax.ppermute(value, axis, [(i, (i + step) % size) for i in range(size)])


def ring(value, step):
    pairs = []
    for x, z, y, core in coordinates():
        there = (x, z, (y + step) % NY, core) if core == 0 else ((x + step) % NX, z, y, core)
        pairs.append((device(x, z, y, core), device(*there)))
    return lax.ppermute(value, ALL, pairs)


def cross(value, step):
    pairs = []
    for x, z, y, core in coordinates():
        there = (x, z, (y + step) % NY, core) if core == 1 else ((x + step) % NX, z, y, core)
        pairs.append((device(x, z, y, core), device(*there)))
    return lax.ppermute(value, ALL, pairs)


def encoder_kernel(*refs):
    pieces, (weight, bias, place, mine, give, rows) = refs[:NY * NC], refs[NY * NC:]
    chunk = pieces[0].shape[0]
    for i, ref in enumerate(pieces):
        rows[i * chunk:(i + 1) * chunk, :] = ref[...]
    preact = jnp.dot(rows[...], weight[...], preferred_element_type=F32) + bias[...]
    activity = jnp.maximum(preact, 0.0).astype(BF)
    mine[...] = jnp.dot(place[0], activity, preferred_element_type=F32).astype(BF)
    give[...] = jnp.dot(place[1], activity, preferred_element_type=F32).astype(BF)


def encode(pieces, weight, bias, place):
    tokens = place.shape[1]
    result = jax.ShapeDtypeStruct((tokens, weight.shape[1]), BF)
    return pl.pallas_call(
        encoder_kernel,
        out_shape=(result, result),
        scratch_shapes=[pltpu.VMEM((tokens, weight.shape[0]), BF)],
        compiler_params=pltpu.CompilerParams(vmem_limit_bytes=VMEM_LIMIT),
        cost_estimate=pl.CostEstimate(flops=8 * 10**8, bytes_accessed=4 * 10**6, transcendentals=0),
        name="encode",
    )(*pieces, weight, bias, place)


def decoder_kernel(where, a0, a1, a2, a3, w0, w1, w2, w3, bias, *refs):
    outs, total = refs[:-1], refs[-1]
    feats = a0.shape[2]
    x, z, y, core = (where[i] for i in range(4))
    adds_bias = (z == 0) & (((core == 0) & (x == y)) | ((core == 1) & (y == 0)))
    value = jnp.where(adds_bias, bias[...], 0.0)
    for i, (a, w) in enumerate(((a0, w0), (a1, w1), (a2, w2), (a3, w3))):
        term = jnp.dot(a[0], w[:feats, :], preferred_element_type=F32)
        term += jnp.dot(a[1], w[feats:2 * feats, :], preferred_element_type=F32)
        value += term if i == 0 else jnp.where((core == 0) | (x >= i), term, 0.0)
    total[...] = jnp.where((core == 1) | (y >= x), value, 0.0)
    first = jnp.where(core == 0, x, y)
    for step, out in enumerate(outs):
        span = total.shape[0] // len(outs)
        start = pl.multiple_of(lax.rem(first + step, len(outs)) * span, span)
        out[...] = total[pl.ds(start, span), :].astype(BF).reshape(out.shape)


def decode(where, acts, weights, bias):
    cores, tokens, feats = acts[0].shape
    rows, width = weights[0].shape
    part, cols = tokens // XZ, 256
    blocks = width // cols
    return pl.pallas_call(
        decoder_kernel,
        grid_spec=pltpu.PrefetchScalarGridSpec(
            num_scalar_prefetch=1,
            grid=(blocks,),
            in_specs=[pl.BlockSpec((cores, tokens, feats), lambda n, _: (0, 0, 0))] * NY
            + [pl.BlockSpec((rows, cols), lambda n, _: (0, n))] * NY
            + [pl.BlockSpec((1, cols), lambda n, where: (0, where[3] * blocks + n))],
            out_specs=[pl.BlockSpec((NZ, part, cols), lambda n, _: (0, 0, n))] * NX,
            scratch_shapes=[pltpu.VMEM((tokens, cols), F32)],
        ),
        out_shape=[jax.ShapeDtypeStruct((NZ, part, width), BF)] * NX,
        compiler_params=pltpu.CompilerParams(vmem_limit_bytes=VMEM_LIMIT),
        cost_estimate=pl.CostEstimate(flops=22 * 10**8, bytes_accessed=8 * 10**6, transcendentals=0),
        name="decode",
    )(where, *acts, *weights, bias)


def sinks_at(where, step):
    x, y, core = where[0], where[2], where[3]
    first, second = jnp.where(core == 0, y, x), jnp.where(core == 0, x, y)
    return lax.rem(first + NY - step, NY), lax.rem(second + NY - step, NY)


def gradient_kernel(step, count, where, *refs):
    own, other, (mine, give), out = refs[:count], refs[count:2 * count], refs[2 * count:2 * count + 2], refs[-1]
    half = pl.program_id(0)
    sinks = sinks_at(where, step)
    for i, (blocks, activity) in enumerate(((own, mine), (other, give))):

        @pl.when((half == i) & (sinks[i] >= where[0]))
        def _():
            grad, start = 0.0, 0
            for block in blocks:
                rhs = block[...].reshape(-1, block.shape[2])
                grad += jnp.dot(activity[:, start:start + rhs.shape[0]], rhs, preferred_element_type=F32)
                start += rhs.shape[0]
            out[0] = grad.astype(BF)

        @pl.when((half == i) & (sinks[i] < where[0]))
        def _():
            out[...] = jnp.zeros(out.shape, BF)


def gradient(step, where, layers, own, other, mine, give, before):
    _, part, cols = own[0].shape
    feats, tokens = mine.shape
    more = [] if before is None else [before]

    def place(half, where):
        first, second = sinks_at(where, step)
        return jnp.where(half == 0, first, second), 0, jnp.where(half == 0, where[3], 1 - where[3])

    return pl.pallas_call(
        functools.partial(gradient_kernel, step, len(own)),
        grid_spec=pltpu.PrefetchScalarGridSpec(
            num_scalar_prefetch=1,
            grid=(NC,),
            in_specs=[pl.BlockSpec((piece.shape[0], part, cols), lambda h, _: (0, 0, 0)) for piece in own] * 2
            + [pl.BlockSpec((feats, tokens), lambda h, _: (0, 0))] * 2
            + [pl.BlockSpec(memory_space=pl.ANY)] * len(more),
            out_specs=pl.BlockSpec((1, feats, cols), place),
        ),
        out_shape=jax.ShapeDtypeStruct((layers, feats, NC * cols), BF),
        input_output_aliases={2 * len(own) + 3: 0} if more else {},
        compiler_params=pltpu.CompilerParams(vmem_limit_bytes=VMEM_LIMIT),
        cost_estimate=pl.CostEstimate(flops=55 * 10**7, bytes_accessed=4 * 10**6, transcendentals=0),
        name="gradient",
    )(where, *own, *other, mine, give, *more)


def collect_kernel(where, *refs):
    pieces, out = refs[:-1], refs[-1]
    first = jnp.where(where[3] == 0, where[0], where[2])
    for step, piece in enumerate(pieces):
        source = lax.rem(first + len(pieces) - step, len(pieces))
        out[pl.ds(source * piece.shape[0], piece.shape[0])] = piece[...]


def collect(where, pieces):
    count, part, width = pieces[0].shape
    cols = width // 2
    return pl.pallas_call(
        collect_kernel,
        grid_spec=pltpu.PrefetchScalarGridSpec(
            num_scalar_prefetch=1,
            grid=(2,),
            in_specs=[pl.BlockSpec((count, part, cols), lambda n, _: (0, 0, n))] * len(pieces),
            out_specs=pl.BlockSpec((count * len(pieces), part, cols), lambda n, _: (0, 0, n)),
        ),
        out_shape=jax.ShapeDtypeStruct((count * len(pieces), part, width), BF),
        compiler_params=pltpu.CompilerParams(vmem_limit_bytes=VMEM_LIMIT),
        cost_estimate=pl.CostEstimate(flops=0, bytes_accessed=2 * 10**6, transcendentals=0),
        name="collect",
    )(where, *pieces)


def pack_kernel(where, own, other, target, out):
    feats = own.shape[1]
    out[:feats, :] = own[0]
    out[feats:2 * feats, :] = other[0]
    out[2 * feats:, :] = target[0]


def pack(step, where, weight, other, target):
    layers, feats, half = other.shape
    extra = target.shape[1]

    def sink(where):
        return lax.rem(jnp.where(where[3] == 0, where[2], where[0]) + step, NY)

    return pl.pallas_call(
        pack_kernel,
        grid_spec=pltpu.PrefetchScalarGridSpec(
            num_scalar_prefetch=1,
            grid=(2,),
            in_specs=[
                pl.BlockSpec((1, feats, half // 2), lambda n, where: (sink(where), 0, where[3] * 2 + n)),
                pl.BlockSpec((1, feats, half // 2), lambda n, where: (sink(where), 0, n)),
                pl.BlockSpec((1, extra, half // 2), lambda n, where: (sink(where), 0, n)),
            ],
            out_specs=pl.BlockSpec((2 * feats + extra, half // 2), lambda n, where: (0, n)),
        ),
        out_shape=jax.ShapeDtypeStruct((2 * feats + extra, half), BF),
        compiler_params=pltpu.CompilerParams(vmem_limit_bytes=VMEM_LIMIT),
        cost_estimate=pl.CostEstimate(flops=0, bytes_accessed=2 * 10**6, transcendentals=0),
        name="pack",
    )(where, weight, other, target)


def body(resid, target, enc_weight, enc_bias, dec_weight, dec_bias):
    x, z, y, core = (lax.axis_index(a) for a in ALL)
    mine, layers, width = resid.shape
    tokens = mine * XZ * NY * NC
    half = width // NC
    factor = 1.0 / math.sqrt(tokens)
    feats = dec_weight.shape[2]
    sink = jnp.where(core == 0, y, x)
    where = jnp.stack([x, z, y, core])

    give = lax.dynamic_slice_in_dim(dec_weight[0], (1 - core) * half, half, axis=2)
    aims = target.transpose(1, 0, 2).reshape(layers, mine, NC, half)
    aims = jnp.where(core == 0, jnp.stack([aims[:, :, 0], aims[:, :, 1]]), jnp.stack([aims[:, :, 1], aims[:, :, 0]]))
    rows = resid.transpose(1, 0, 2)
    rows, give, aims, where = lax.optimization_barrier((rows, give, aims, where))
    extra = jnp.concatenate([aims[0], shift(aims[1], "c", 1), jnp.zeros((layers, 16 - 2 * mine, half), BF)], axis=1)
    give = shift(give, "c", 1)
    weights = [pack(step, where, dec_weight[0], give, extra) for step in range(NY)]
    rows = lax.all_to_all(rows, "x", 0, 0, tiled=True)
    rows, *sent = lax.optimization_barrier((rows, *weights[1:]))
    weights = weights[:1] + [ring(piece, step) for step, piece in enumerate(sent, 1)]
    rows = jnp.broadcast_to(rows.reshape(1, layers * mine, width), (NZ, layers * mine, width))
    rows = lax.all_to_all(rows, "z", 0, 0, tiled=True).reshape(XZ * mine, width)
    rows, w1, w3 = lax.optimization_barrier((rows, weights[1], weights[3]))
    weights = [weights[0], w1, weights[2], w3]
    pieces = [rows] + [shift(rows, "y", step) for step in range(1, NY)]
    pieces = pieces + [shift(piece, "c", 1) for piece in pieces]
    r = jnp.arange(tokens)
    r_core = jnp.where(r // (tokens // 2) == 0, core, 1 - core)
    r_y = (y + NY - r // (tokens // 8) % NY) % NY
    r_x, r_z, r_i = r // mine % NX, r // (mine * NX) % NZ, r % mine
    order = [((a * NZ + r_z) * 4 + b) * NC * mine + r_core * mine + r_i for a, b in ((r_x, r_y), (r_y, r_x))]
    order = jnp.stack([jnp.where(core == 0, order[0], order[1]), jnp.where(core == 0, order[1], order[0])])
    place = (jnp.arange(tokens)[None, :, None] == order[:, None, :]).astype(BF)
    own, away = encode(pieces, enc_weight[0], enc_bias, place)

    act = jnp.stack([own, shift(away, "c", 1)])
    acts = [act] + [ring(act, step) for step in range(1, NY)]
    parts = decode(where, acts, weights, dec_bias)

    wanted = jnp.concatenate([w[2 * feats:2 * feats + 2 * mine] for w in weights])
    q = jnp.arange(NY * NC * mine)
    q_core = jnp.where(q // mine % NC == 0, core, 1 - core)
    q = (sink + NY - q // (NC * mine)) % NY * NC * mine + q_core * mine + q % mine
    wanted = jnp.dot((jnp.arange(q.shape[0])[:, None] == q[None, :]).astype(BF), wanted, preferred_element_type=F32)

    parts = [part if step == 0 else cross(part, step) for step, part in enumerate(parts)]
    own, away = own.T, away.T
    *parts, own, away = lax.optimization_barrier((*parts, own, away))
    total = sum(part.astype(F32) for part in parts).astype(BF)
    got = lax.all_to_all(total, "z", 0, 0, tiled=True)
    misfit = jnp.sum(got.astype(F32), axis=0) - wanted
    cotangent = (misfit * factor).astype(BF)

    block = lax.all_to_all(jnp.broadcast_to(cotangent[None], (NZ,) + cotangent.shape), "z", 0, 0, tiled=True)
    block = collect(where, [block] + [cross(block, step) for step in range(1, NX)])
    before, after = ring(block, 1), ring(block, 3)
    middle = XZ // 2
    far = [ring(after[:middle], 3), ring(before[middle:], 1)]
    grads = None
    for step, pieces in ((0, [block]), (1, [before]), (3, [after]), (2, far)):
        if step == 2:
            *pieces, grads = lax.optimization_barrier((*pieces, grads))
        others = [shift(piece, "c", 1) for piece in pieces]
        grads = gradient(step, where, layers, pieces, others, own, away, grads)
    return grads[None]


def solution(mesh):
    fine = Mesh(mesh.devices.reshape(NX, NZ, NY, NC), ("x", "z", "y", "c"))
    feat = ("z", "y", "c")
    return jax.shard_map(
        body,
        mesh=fine,
        in_specs=(
            P(("x",) + feat, None, None),
            P(("x",) + feat, None, None),
            P("x", None, feat),
            P("x", feat),
            P("x", None, feat, None),
            P("x", None),
        ),
        out_specs=P("x", None, feat, None),
        check_vma=False,
    )
```

```python
import functools
import math

import jax
import jax.numpy as jnp
from jax import lax
from jax.experimental import pallas as pl
from jax.experimental.pallas import tpu as pltpu
from jax.sharding import Mesh
from jax.sharding import PartitionSpec as P

BF = jnp.bfloat16
F32 = jnp.float32
NX, NZ, NY, NC = 4, 8, 4, 2
XZ = NX * NZ

ALL = ("x", "z", "y", "c")
VMEM_LIMIT = 24 * 1024 * 1024


def device(x, z, y, core):
    return ((x * NZ + z) * NY + y) * NC + core


def coordinates():
    return [(x, z, y, core) for x in range(NX) for z in range(NZ) for y in range(NY) for core in range(NC)]


def shift(value, axis, step):
    size = lax.axis_size(axis)
    return lax.ppermute(value, axis, [(i, (i + step) % size) for i in range(size)])


def ring(value, step):
    pairs = []
    for x, z, y, core in coordinates():
        there = (x, z, (y + step) % NY, core) if core == 0 else ((x + step) % NX, z, y, core)
        pairs.append((device(x, z, y, core), device(*there)))
    return lax.ppermute(value, ALL, pairs)


def cross(value, step):
    pairs = []
    for x, z, y, core in coordinates():
        there = (x, z, (y + step) % NY, core) if core == 1 else ((x + step) % NX, z, y, core)
        pairs.append((device(x, z, y, core), device(*there)))
    return lax.ppermute(value, ALL, pairs)


def encoder_kernel(*refs):
    pieces, (weight, bias, place, mine, give, rows) = refs[:NY * NC], refs[NY * NC:]
    chunk = pieces[0].shape[0]
    for i, ref in enumerate(pieces):
        rows[i * chunk:(i + 1) * chunk, :] = ref[...]
    preact = jnp.dot(rows[...], weight[...], preferred_element_type=F32) + bias[...]
    activity = jnp.maximum(preact, 0.0).astype(BF)
    mine[...] = jnp.dot(place[0], activity, preferred_element_type=F32).astype(BF)
    give[...] = jnp.dot(place[1], activity, preferred_element_type=F32).astype(BF)


def encode(pieces, weight, bias, place):
    tokens = place.shape[1]
    result = jax.ShapeDtypeStruct((tokens, weight.shape[1]), BF)
    return pl.pallas_call(
        encoder_kernel,
        out_shape=(result, result),
        scratch_shapes=[pltpu.VMEM((tokens, weight.shape[0]), BF)],
        compiler_params=pltpu.CompilerParams(vmem_limit_bytes=VMEM_LIMIT),
        cost_estimate=pl.CostEstimate(flops=8 * 10**8, bytes_accessed=4 * 10**6, transcendentals=0),
        name="encode",
    )(*pieces, weight, bias, place)


def products(where, steps, acts, weights):
    x, core = where[0], where[3]
    value = 0.0
    for step, a, w in zip(steps, acts, weights):
        feats = a.shape[2]
        term = jnp.dot(a[0], w[:feats, :], preferred_element_type=F32)
        term += jnp.dot(a[1], w[feats:2 * feats, :], preferred_element_type=F32)
        value += term if step == 0 else jnp.where((core == 0) | (x >= step), term, 0.0)
    return value


def early_kernel(steps, where, *refs):
    count = len(steps)
    acts, weights, (bias, out) = refs[:count], refs[count:2 * count], refs[2 * count:]
    x, z, y, core = (where[i] for i in range(4))
    adds_bias = (z == 0) & (((core == 0) & (x == y)) | ((core == 1) & (y == 0)))
    out[...] = jnp.where(adds_bias, bias[...], 0.0) + products(where, steps, acts, weights)


def late_kernel(steps, where, *refs):
    count = len(steps)
    acts, weights, early, outs, total = refs[:count], refs[count:2 * count], refs[2 * count], refs[2 * count + 1:-1], refs[-1]
    x, y, core = where[0], where[2], where[3]
    value = early[...] + products(where, steps, acts, weights)
    total[...] = jnp.where((core == 1) | (y >= x), value, 0.0)
    first = jnp.where(core == 0, x, y)
    for step, out in enumerate(outs):
        span = total.shape[0] // len(outs)
        start = pl.multiple_of(lax.rem(first + step, len(outs)) * span, span)
        out[...] = total[pl.ds(start, span), :].astype(BF).reshape(out.shape)


def decode(steps, where, acts, weights, bias=None, early=None):
    acts, weights = [acts[step] for step in steps], [weights[step] for step in steps]
    cores, tokens, feats = acts[0].shape
    rows, width = weights[0].shape
    part, cols = tokens // XZ, 256
    blocks = width // cols
    if early is None:
        kernel, last = early_kernel, bias
        last_spec = pl.BlockSpec((1, cols), lambda n, where: (0, where[3] * blocks + n))
        out_specs = pl.BlockSpec((tokens, cols), lambda n, _: (0, n))
        out_shape, scratch = jax.ShapeDtypeStruct((tokens, width), F32), []
    else:
        kernel, last = late_kernel, early
        last_spec = pl.BlockSpec((tokens, cols), lambda n, _: (0, n))
        out_specs = [pl.BlockSpec((NZ, part, cols), lambda n, _: (0, 0, n))] * NX
        out_shape, scratch = [jax.ShapeDtypeStruct((NZ, part, width), BF)] * NX, [pltpu.VMEM((tokens, cols), F32)]
    return pl.pallas_call(
        functools.partial(kernel, steps),
        grid_spec=pltpu.PrefetchScalarGridSpec(
            num_scalar_prefetch=1,
            grid=(blocks,),
            in_specs=[pl.BlockSpec((cores, tokens, feats), lambda n, _: (0, 0, 0))] * len(steps)
            + [pl.BlockSpec((rows, cols), lambda n, _: (0, n))] * len(steps)
            + [last_spec],
            out_specs=out_specs,
            scratch_shapes=scratch,
        ),
        out_shape=out_shape,
        compiler_params=pltpu.CompilerParams(vmem_limit_bytes=VMEM_LIMIT),
        cost_estimate=pl.CostEstimate(flops=55 * 10**7 * len(steps), bytes_accessed=4 * 10**6, transcendentals=0),
        name="decode",
    )(where, *acts, *weights, last)


def sinks_at(where, step):
    x, y, core = where[0], where[2], where[3]
    first, second = jnp.where(core == 0, y, x), jnp.where(core == 0, x, y)
    return lax.rem(first + NY - step, NY), lax.rem(second + NY - step, NY)


def gradient_kernel(step, halves, count, where, *refs):
    (mine, give), out = refs[count * len(halves):count * len(halves) + 2], refs[-1]
    half = pl.program_id(0) + halves[0]
    sinks = sinks_at(where, step)
    for k, i in enumerate(halves):
        blocks, activity = refs[k * count:(k + 1) * count], (mine, give)[i]

        @pl.when((half == i) & (sinks[i] >= where[0]))
        def _():
            grad, start = 0.0, 0
            for block in blocks:
                rhs = block[...].reshape(-1, block.shape[2])
                grad += jnp.dot(activity[:, start:start + rhs.shape[0]], rhs, preferred_element_type=F32)
                start += rhs.shape[0]
            out[0] = grad.astype(BF)

        @pl.when((half == i) & (sinks[i] < where[0]))
        def _():
            out[...] = jnp.zeros(out.shape, BF)


def gradient(step, where, layers, given, mine, give, before):
    halves = tuple(sorted(given))
    pieces = [piece for i in halves for piece in given[i]]
    count = len(pieces) // len(halves)
    _, part, cols = pieces[0].shape
    feats, tokens = mine.shape
    more = [] if before is None else [before]

    def place(half, where):
        half = half + halves[0]
        first, second = sinks_at(where, step)
        return jnp.where(half == 0, first, second), 0, jnp.where(half == 0, where[3], 1 - where[3])

    return pl.pallas_call(
        functools.partial(gradient_kernel, step, halves, count),
        grid_spec=pltpu.PrefetchScalarGridSpec(
            num_scalar_prefetch=1,
            grid=(len(halves),),
            in_specs=[pl.BlockSpec((piece.shape[0], part, cols), lambda h, _: (0, 0, 0)) for piece in pieces]
            + [pl.BlockSpec((feats, tokens), lambda h, _: (0, 0))] * 2
            + [pl.BlockSpec(memory_space=pl.ANY)] * len(more),
            out_specs=pl.BlockSpec((1, feats, cols), place),
        ),
        out_shape=jax.ShapeDtypeStruct((layers, feats, NC * cols), BF),
        input_output_aliases={len(pieces) + 3: 0} if more else {},
        compiler_params=pltpu.CompilerParams(vmem_limit_bytes=VMEM_LIMIT),
        cost_estimate=pl.CostEstimate(flops=55 * 10**7, bytes_accessed=4 * 10**6, transcendentals=0),
        name="gradient",
    )(where, *pieces, mine, give, *more)


def collect_kernel(where, *refs):
    pieces, out = refs[:-1], refs[-1]
    first = jnp.where(where[3] == 0, where[0], where[2])
    for step, piece in enumerate(pieces):
        source = lax.rem(first + len(pieces) - step, len(pieces))
        out[pl.ds(source * piece.shape[0], piece.shape[0])] = piece[...]


def collect(where, pieces):
    count, part, width = pieces[0].shape
    cols = width // 2
    return pl.pallas_call(
        collect_kernel,
        grid_spec=pltpu.PrefetchScalarGridSpec(
            num_scalar_prefetch=1,
            grid=(2,),
            in_specs=[pl.BlockSpec((count, part, cols), lambda n, _: (0, 0, n))] * len(pieces),
            out_specs=pl.BlockSpec((count * len(pieces), part, cols), lambda n, _: (0, 0, n)),
        ),
        out_shape=jax.ShapeDtypeStruct((count * len(pieces), part, width), BF),
        compiler_params=pltpu.CompilerParams(vmem_limit_bytes=VMEM_LIMIT),
        cost_estimate=pl.CostEstimate(flops=0, bytes_accessed=2 * 10**6, transcendentals=0),
        name="collect",
    )(where, *pieces)


def pack_kernel(where, own, other, target, out):
    feats = own.shape[1]
    out[:feats, :] = own[0]
    out[feats:2 * feats, :] = other[0]
    out[2 * feats:, :] = target[0]


def pack(step, where, weight, other, target):
    layers, feats, half = other.shape
    extra = target.shape[1]

    def sink(where):
        return lax.rem(jnp.where(where[3] == 0, where[2], where[0]) + step, NY)

    return pl.pallas_call(
        pack_kernel,
        grid_spec=pltpu.PrefetchScalarGridSpec(
            num_scalar_prefetch=1,
            grid=(2,),
            in_specs=[
                pl.BlockSpec((1, feats, half // 2), lambda n, where: (sink(where), 0, where[3] * 2 + n)),
                pl.BlockSpec((1, feats, half // 2), lambda n, where: (sink(where), 0, n)),
                pl.BlockSpec((1, extra, half // 2), lambda n, where: (sink(where), 0, n)),
            ],
            out_specs=pl.BlockSpec((2 * feats + extra, half // 2), lambda n, where: (0, n)),
        ),
        out_shape=jax.ShapeDtypeStruct((2 * feats + extra, half), BF),
        compiler_params=pltpu.CompilerParams(vmem_limit_bytes=VMEM_LIMIT),
        cost_estimate=pl.CostEstimate(flops=0, bytes_accessed=2 * 10**6, transcendentals=0),
        name="pack",
    )(where, weight, other, target)


def body(resid, target, enc_weight, enc_bias, dec_weight, dec_bias):
    x, z, y, core = (lax.axis_index(a) for a in ALL)
    mine, layers, width = resid.shape
    tokens = mine * XZ * NY * NC
    half = width // NC
    factor = 1.0 / math.sqrt(tokens)
    feats = dec_weight.shape[2]
    sink = jnp.where(core == 0, y, x)
    where = jnp.stack([x, z, y, core])

    give = lax.dynamic_slice_in_dim(dec_weight[0], (1 - core) * half, half, axis=2)
    aims = target.transpose(1, 0, 2).reshape(layers, mine, NC, half)
    aims = jnp.where(core == 0, jnp.stack([aims[:, :, 0], aims[:, :, 1]]), jnp.stack([aims[:, :, 1], aims[:, :, 0]]))
    rows = resid.transpose(1, 0, 2)
    rows, give, aims, where = lax.optimization_barrier((rows, give, aims, where))
    extra = jnp.concatenate([aims[0], shift(aims[1], "c", 1), jnp.zeros((layers, 16 - 2 * mine, half), BF)], axis=1)
    give = shift(give, "c", 1)
    weights = [pack(step, where, dec_weight[0], give, extra) for step in range(NY)]
    rows = lax.all_to_all(rows, "x", 0, 0, tiled=True)
    rows, *sent = lax.optimization_barrier((rows, *weights[1:]))
    weights = weights[:1] + [ring(piece, step) for step, piece in enumerate(sent, 1)]
    rows = jnp.broadcast_to(rows.reshape(1, layers * mine, width), (NZ, layers * mine, width))
    rows = lax.all_to_all(rows, "z", 0, 0, tiled=True).reshape(XZ * mine, width)
    rows, w1, w3 = lax.optimization_barrier((rows, weights[1], weights[3]))
    weights = [weights[0], w1, weights[2], w3]
    pieces = [rows] + [shift(rows, "y", step) for step in range(1, NY)]
    pieces = pieces + [shift(piece, "c", 1) for piece in pieces]
    r = jnp.arange(tokens)
    r_core = jnp.where(r // (tokens // 2) == 0, core, 1 - core)
    r_y = (y + NY - r // (tokens // 8) % NY) % NY
    r_x, r_z, r_i = r // mine % NX, r // (mine * NX) % NZ, r % mine
    order = [((a * NZ + r_z) * 4 + b) * NC * mine + r_core * mine + r_i for a, b in ((r_x, r_y), (r_y, r_x))]
    order = jnp.stack([jnp.where(core == 0, order[0], order[1]), jnp.where(core == 0, order[1], order[0])])
    place = (jnp.arange(tokens)[None, :, None] == order[:, None, :]).astype(BF)
    own, away = encode(pieces, enc_weight[0], enc_bias, place)

    act = jnp.stack([own, shift(away, "c", 1)])
    acts = [act] + [ring(act, step) for step in range(1, NY)]
    early = decode((0, 1, 3), where, acts, weights, bias=dec_bias)
    acts[2], early = lax.optimization_barrier((acts[2], early))
    parts = decode((2,), where, acts, weights, early=early)

    wanted = jnp.concatenate([w[2 * feats:2 * feats + 2 * mine] for w in weights])
    q = jnp.arange(NY * NC * mine)
    q_core = jnp.where(q // mine % NC == 0, core, 1 - core)
    q = (sink + NY - q // (NC * mine)) % NY * NC * mine + q_core * mine + q % mine
    wanted = jnp.dot((jnp.arange(q.shape[0])[:, None] == q[None, :]).astype(BF), wanted, preferred_element_type=F32)

    parts = [part if step == 0 else cross(part, step) for step, part in enumerate(parts)]
    own, away = own.T, away.T
    *parts, own, away = lax.optimization_barrier((*parts, own, away))
    total = sum(part.astype(F32) for part in parts).astype(BF)
    got = lax.all_to_all(total, "z", 0, 0, tiled=True)
    misfit = jnp.sum(got.astype(F32), axis=0) - wanted
    cotangent = (misfit * factor).astype(BF)

    block = lax.all_to_all(jnp.broadcast_to(cotangent[None], (NZ,) + cotangent.shape), "z", 0, 0, tiled=True)
    block = collect(where, [block] + [cross(block, step) for step in range(1, NX)])
    before, after = ring(block, 1), ring(block, 3)
    middle = XZ // 2
    far = [ring(after[:middle], 3), ring(before[middle:], 1)]
    grads = None
    for step, pieces in ((0, [block]), (1, [before]), (3, [after])):
        given = {0: pieces, 1: [shift(piece, "c", 1) for piece in pieces]}
        grads = gradient(step, where, layers, given, own, away, grads)
    *far, grads = lax.optimization_barrier((*far, grads))
    others = [shift(piece, "c", 1) for piece in far]
    grads = gradient(2, where, layers, {0: far}, own, away, grads)
    grads = gradient(2, where, layers, {1: others}, own, away, grads)
    return grads[None]


def solution(mesh):
    fine = Mesh(mesh.devices.reshape(NX, NZ, NY, NC), ("x", "z", "y", "c"))
    feat = ("z", "y", "c")
    return jax.shard_map(
        body,
        mesh=fine,
        in_specs=(
            P(("x",) + feat, None, None),
            P(("x",) + feat, None, None),
            P("x", None, feat),
            P("x", feat),
            P("x", None, feat, None),
            P("x", None),
        ),
        out_specs=P("x", None, feat, None),
        check_vma=False,
    )
```

```python
import functools
import math

import jax
import jax.numpy as jnp
from jax import lax
from jax.experimental import pallas as pl
from jax.experimental.pallas import tpu as pltpu
from jax.sharding import Mesh
from jax.sharding import PartitionSpec as P

BF = jnp.bfloat16
F32 = jnp.float32
NX, NZ, NY, NC = 4, 8, 4, 2
XZ = NX * NZ

ALL = ("x", "z", "y", "c")
VMEM_LIMIT = 24 * 1024 * 1024


def device(x, z, y, core):
    return ((x * NZ + z) * NY + y) * NC + core


def coordinates():
    return [(x, z, y, core) for x in range(NX) for z in range(NZ) for y in range(NY) for core in range(NC)]


def shift(value, axis, step):
    size = lax.axis_size(axis)
    return lax.ppermute(value, axis, [(i, (i + step) % size) for i in range(size)])


def ring(value, step):
    pairs = []
    for x, z, y, core in coordinates():
        there = (x, z, (y + step) % NY, core) if core == 0 else ((x + step) % NX, z, y, core)
        pairs.append((device(x, z, y, core), device(*there)))
    return lax.ppermute(value, ALL, pairs)


def cross(value, step):
    pairs = []
    for x, z, y, core in coordinates():
        there = (x, z, (y + step) % NY, core) if core == 1 else ((x + step) % NX, z, y, core)
        pairs.append((device(x, z, y, core), device(*there)))
    return lax.ppermute(value, ALL, pairs)


def encoder_kernel(*refs):
    pieces, (weight, bias, place, mine, give, rows) = refs[:NY * NC], refs[NY * NC:]
    chunk = pieces[0].shape[0]
    for i, ref in enumerate(pieces):
        rows[i * chunk:(i + 1) * chunk, :] = ref[...]
    preact = jnp.dot(rows[...], weight[...], preferred_element_type=F32) + bias[...]
    activity = jnp.maximum(preact, 0.0).astype(BF)
    mine[...] = jnp.dot(place[0], activity, preferred_element_type=F32).astype(BF)
    give[...] = jnp.dot(place[1], activity, preferred_element_type=F32).astype(BF)


def encode(pieces, weight, bias, place):
    tokens = place.shape[1]
    result = jax.ShapeDtypeStruct((tokens, weight.shape[1]), BF)
    return pl.pallas_call(
        encoder_kernel,
        out_shape=(result, result),
        scratch_shapes=[pltpu.VMEM((tokens, weight.shape[0]), BF)],
        compiler_params=pltpu.CompilerParams(vmem_limit_bytes=VMEM_LIMIT),
        cost_estimate=pl.CostEstimate(flops=8 * 10**8, bytes_accessed=4 * 10**6, transcendentals=0),
        name="encode",
    )(*pieces, weight, bias, place)


def products(where, steps, acts, weights):
    x, core = where[0], where[3]
    value = 0.0
    for step, a, w in zip(steps, acts, weights):
        feats = a.shape[2]
        term = jnp.dot(a[0], w[:feats, :], preferred_element_type=F32)
        term += jnp.dot(a[1], w[feats:2 * feats, :], preferred_element_type=F32)
        value += term if step == 0 else jnp.where((core == 0) | (x >= step), term, 0.0)
    return value


def early_kernel(steps, where, *refs):
    count = len(steps)
    acts, weights, (bias, out) = refs[:count], refs[count:2 * count], refs[2 * count:]
    x, z, y, core = (where[i] for i in range(4))
    adds_bias = (z == 0) & (((core == 0) & (x == y)) | ((core == 1) & (y == 0)))
    out[...] = jnp.where(adds_bias, bias[...], 0.0) + products(where, steps, acts, weights)


def late_kernel(steps, where, *refs):
    count = len(steps)
    acts, weights, early, outs, total = refs[:count], refs[count:2 * count], refs[2 * count], refs[2 * count + 1:-1], refs[-1]
    x, y, core = where[0], where[2], where[3]
    value = early[...] + products(where, steps, acts, weights)
    total[...] = jnp.where((core == 1) | (y >= x), value, 0.0)
    first = jnp.where(core == 0, x, y)
    for step, out in enumerate(outs):
        span = total.shape[0] // len(outs)
        start = pl.multiple_of(lax.rem(first + step, len(outs)) * span, span)
        out[...] = total[pl.ds(start, span), :].astype(BF).reshape(out.shape)


def decode(steps, where, acts, weights, bias=None, early=None):
    acts, weights = [acts[step] for step in steps], [weights[step] for step in steps]
    cores, tokens, feats = acts[0].shape
    rows, width = weights[0].shape
    part, cols = tokens // XZ, 256
    blocks = width // cols
    if early is None:
        kernel, last = early_kernel, bias
        last_spec = pl.BlockSpec((1, cols), lambda n, where: (0, where[3] * blocks + n))
        out_specs = pl.BlockSpec((tokens, cols), lambda n, _: (0, n))
        out_shape, scratch = jax.ShapeDtypeStruct((tokens, width), F32), []
    else:
        kernel, last = late_kernel, early
        last_spec = pl.BlockSpec((tokens, cols), lambda n, _: (0, n))
        out_specs = [pl.BlockSpec((NZ, part, cols), lambda n, _: (0, 0, n))] * NX
        out_shape, scratch = [jax.ShapeDtypeStruct((NZ, part, width), BF)] * NX, [pltpu.VMEM((tokens, cols), F32)]
    return pl.pallas_call(
        functools.partial(kernel, steps),
        grid_spec=pltpu.PrefetchScalarGridSpec(
            num_scalar_prefetch=1,
            grid=(blocks,),
            in_specs=[pl.BlockSpec((cores, tokens, feats), lambda n, _: (0, 0, 0))] * len(steps)
            + [pl.BlockSpec((rows, cols), lambda n, _: (0, n))] * len(steps)
            + [last_spec],
            out_specs=out_specs,
            scratch_shapes=scratch,
        ),
        out_shape=out_shape,
        compiler_params=pltpu.CompilerParams(vmem_limit_bytes=VMEM_LIMIT),
        cost_estimate=pl.CostEstimate(flops=55 * 10**7 * len(steps), bytes_accessed=4 * 10**6, transcendentals=0),
        name="decode",
    )(where, *acts, *weights, last)


def sinks_at(where, step):
    x, y, core = where[0], where[2], where[3]
    first, second = jnp.where(core == 0, y, x), jnp.where(core == 0, x, y)
    return lax.rem(first + NY - step, NY), lax.rem(second + NY - step, NY)


def gradient_kernel(step, halves, count, where, *refs):
    (mine, give), out = refs[count * len(halves):count * len(halves) + 2], refs[-1]
    half = pl.program_id(0) + halves[0]
    sinks = sinks_at(where, step)
    for k, i in enumerate(halves):
        blocks, activity = refs[k * count:(k + 1) * count], (mine, give)[i]

        @pl.when((half == i) & (sinks[i] >= where[0]))
        def _():
            grad, start = 0.0, 0
            for block in blocks:
                rhs = block[...].reshape(-1, block.shape[2])
                grad += jnp.dot(activity[:, start:start + rhs.shape[0]], rhs, preferred_element_type=F32)
                start += rhs.shape[0]
            out[0] = grad.astype(BF)

        @pl.when((half == i) & (sinks[i] < where[0]))
        def _():
            out[...] = jnp.zeros(out.shape, BF)


def gradient(step, where, layers, given, mine, give, before):
    halves = tuple(sorted(given))
    pieces = [piece for i in halves for piece in given[i]]
    count = len(pieces) // len(halves)
    _, part, cols = pieces[0].shape
    feats, tokens = mine.shape
    more = [] if before is None else [before]

    def place(half, where):
        half = half + halves[0]
        first, second = sinks_at(where, step)
        return jnp.where(half == 0, first, second), 0, jnp.where(half == 0, where[3], 1 - where[3])

    return pl.pallas_call(
        functools.partial(gradient_kernel, step, halves, count),
        grid_spec=pltpu.PrefetchScalarGridSpec(
            num_scalar_prefetch=1,
            grid=(len(halves),),
            in_specs=[pl.BlockSpec((piece.shape[0], part, cols), lambda h, _: (0, 0, 0)) for piece in pieces]
            + [pl.BlockSpec((feats, tokens), lambda h, _: (0, 0))] * 2
            + [pl.BlockSpec(memory_space=pl.ANY)] * len(more),
            out_specs=pl.BlockSpec((1, feats, cols), place),
        ),
        out_shape=jax.ShapeDtypeStruct((layers, feats, NC * cols), BF),
        input_output_aliases={len(pieces) + 3: 0} if more else {},
        compiler_params=pltpu.CompilerParams(vmem_limit_bytes=VMEM_LIMIT),
        cost_estimate=pl.CostEstimate(flops=55 * 10**7, bytes_accessed=4 * 10**6, transcendentals=0),
        name="gradient",
    )(where, *pieces, mine, give, *more)


def collect_kernel(where, *refs):
    pieces, out = refs[:-1], refs[-1]
    first = jnp.where(where[3] == 0, where[0], where[2])
    for step, piece in enumerate(pieces):
        source = lax.rem(first + len(pieces) - step, len(pieces))
        out[pl.ds(source * piece.shape[0], piece.shape[0])] = piece[...]


def collect(where, pieces):
    count, part, width = pieces[0].shape
    cols = width // 2
    return pl.pallas_call(
        collect_kernel,
        grid_spec=pltpu.PrefetchScalarGridSpec(
            num_scalar_prefetch=1,
            grid=(2,),
            in_specs=[pl.BlockSpec((count, part, cols), lambda n, _: (0, 0, n))] * len(pieces),
            out_specs=pl.BlockSpec((count * len(pieces), part, cols), lambda n, _: (0, 0, n)),
        ),
        out_shape=jax.ShapeDtypeStruct((count * len(pieces), part, width), BF),
        compiler_params=pltpu.CompilerParams(vmem_limit_bytes=VMEM_LIMIT),
        cost_estimate=pl.CostEstimate(flops=0, bytes_accessed=2 * 10**6, transcendentals=0),
        name="collect",
    )(where, *pieces)


def pack_kernel(where, *refs):
    outs = refs[3 * len(refs) // 4:]
    for i, out in enumerate(outs):
        own, other, target = refs[3 * i:3 * i + 3]
        feats = own.shape[1]
        out[:feats, :] = own[0]
        out[feats:2 * feats, :] = other[0]
        out[2 * feats:, :] = target[0]


def pack(steps, where, weight, other, target):
    layers, feats, half = other.shape
    extra = target.shape[1]
    in_specs = []
    for step in steps:

        def sink(where, step=step):
            return lax.rem(jnp.where(where[3] == 0, where[2], where[0]) + step, NY)

        in_specs += [
            pl.BlockSpec((1, feats, half // 2), lambda n, where, sink=sink: (sink(where), 0, where[3] * 2 + n)),
            pl.BlockSpec((1, feats, half // 2), lambda n, where, sink=sink: (sink(where), 0, n)),
            pl.BlockSpec((1, extra, half // 2), lambda n, where, sink=sink: (sink(where), 0, n)),
        ]
    return pl.pallas_call(
        pack_kernel,
        grid_spec=pltpu.PrefetchScalarGridSpec(
            num_scalar_prefetch=1,
            grid=(2,),
            in_specs=in_specs,
            out_specs=[pl.BlockSpec((2 * feats + extra, half // 2), lambda n, where: (0, n))] * len(steps),
        ),
        out_shape=[jax.ShapeDtypeStruct((2 * feats + extra, half), BF)] * len(steps),
        compiler_params=pltpu.CompilerParams(vmem_limit_bytes=VMEM_LIMIT),
        cost_estimate=pl.CostEstimate(flops=0, bytes_accessed=2 * 10**6 * len(steps), transcendentals=0),
        name="pack",
    )(where, *([weight, other, target] * len(steps)))


def body(resid, target, enc_weight, enc_bias, dec_weight, dec_bias):
    x, z, y, core = (lax.axis_index(a) for a in ALL)
    mine, layers, width = resid.shape
    tokens = mine * XZ * NY * NC
    half = width // NC
    factor = 1.0 / math.sqrt(tokens)
    feats = dec_weight.shape[2]
    sink = jnp.where(core == 0, y, x)
    where = jnp.stack([x, z, y, core])

    give = lax.dynamic_slice_in_dim(dec_weight[0], (1 - core) * half, half, axis=2)
    aims = target.transpose(1, 0, 2).reshape(layers, mine, NC, half)
    aims = jnp.where(core == 0, jnp.stack([aims[:, :, 0], aims[:, :, 1]]), jnp.stack([aims[:, :, 1], aims[:, :, 0]]))
    rows = resid.transpose(1, 0, 2)
    rows, give, aims, where = lax.optimization_barrier((rows, give, aims, where))
    extra = jnp.concatenate([aims[0], shift(aims[1], "c", 1), jnp.zeros((layers, 16 - 2 * mine, half), BF)], axis=1)
    give = shift(give, "c", 1)
    weights = [*pack((0,), where, dec_weight[0], give, extra), *pack((1, 2, 3), where, dec_weight[0], give, extra)]
    rows = lax.all_to_all(rows, "x", 0, 0, tiled=True)
    rows, *sent = lax.optimization_barrier((rows, *weights[1:]))
    weights = weights[:1] + [ring(piece, step) for step, piece in enumerate(sent, 1)]
    rows = jnp.broadcast_to(rows.reshape(1, layers * mine, width), (NZ, layers * mine, width))
    rows = lax.all_to_all(rows, "z", 0, 0, tiled=True).reshape(XZ * mine, width)
    rows, w1, w3 = lax.optimization_barrier((rows, weights[1], weights[3]))
    weights = [weights[0], w1, weights[2], w3]
    pieces = [rows] + [shift(rows, "y", step) for step in range(1, NY)]
    pieces = pieces + [shift(piece, "c", 1) for piece in pieces]
    r = jnp.arange(tokens)
    r_core = jnp.where(r // (tokens // 2) == 0, core, 1 - core)
    r_y = (y + NY - r // (tokens // 8) % NY) % NY
    r_x, r_z, r_i = r // mine % NX, r // (mine * NX) % NZ, r % mine
    order = [((a * NZ + r_z) * 4 + b) * NC * mine + r_core * mine + r_i for a, b in ((r_x, r_y), (r_y, r_x))]
    order = jnp.stack([jnp.where(core == 0, order[0], order[1]), jnp.where(core == 0, order[1], order[0])])
    place = (jnp.arange(tokens)[None, :, None] == order[:, None, :]).astype(BF)
    own, away = encode(pieces, enc_weight[0], enc_bias, place)

    act = jnp.stack([own, shift(away, "c", 1)])
    acts = [act] + [ring(act, step) for step in range(1, NY)]
    early = decode((0, 1, 3), where, acts, weights, bias=dec_bias)
    acts[2], early = lax.optimization_barrier((acts[2], early))
    parts = decode((2,), where, acts, weights, early=early)

    wanted = jnp.concatenate([w[2 * feats:2 * feats + 2 * mine] for w in weights])
    q = jnp.arange(NY * NC * mine)
    q_core = jnp.where(q // mine % NC == 0, core, 1 - core)
    q = (sink + NY - q // (NC * mine)) % NY * NC * mine + q_core * mine + q % mine
    wanted = jnp.dot((jnp.arange(q.shape[0])[:, None] == q[None, :]).astype(BF), wanted, preferred_element_type=F32)

    parts = [part if step == 0 else cross(part, step) for step, part in enumerate(parts)]
    own, away = own.T, away.T
    *parts, own, away = lax.optimization_barrier((*parts, own, away))
    total = sum(part.astype(F32) for part in parts).astype(BF)
    got = lax.all_to_all(total, "z", 0, 0, tiled=True)
    misfit = jnp.sum(got.astype(F32), axis=0) - wanted
    cotangent = (misfit * factor).astype(BF)

    block = lax.all_to_all(jnp.broadcast_to(cotangent[None], (NZ,) + cotangent.shape), "z", 0, 0, tiled=True)
    block = collect(where, [block] + [cross(block, step) for step in range(1, NX)])
    before, after = ring(block, 1), ring(block, 3)
    middle = XZ // 2
    far = [ring(after[:middle], 3), ring(before[middle:], 1)]
    grads = None
    for step, pieces in ((0, [block]), (1, [before]), (3, [after])):
        given = {0: pieces, 1: [shift(piece, "c", 1) for piece in pieces]}
        grads = gradient(step, where, layers, given, own, away, grads)
    *far, grads = lax.optimization_barrier((*far, grads))
    others = [shift(piece, "c", 1) for piece in far]
    grads = gradient(2, where, layers, {0: far}, own, away, grads)
    grads = gradient(2, where, layers, {1: others}, own, away, grads)
    return grads[None]


def solution(mesh):
    fine = Mesh(mesh.devices.reshape(NX, NZ, NY, NC), ("x", "z", "y", "c"))
    feat = ("z", "y", "c")
    return jax.shard_map(
        body,
        mesh=fine,
        in_specs=(
            P(("x",) + feat, None, None),
            P(("x",) + feat, None, None),
            P("x", None, feat),
            P("x", feat),
            P("x", None, feat, None),
            P("x", None),
        ),
        out_specs=P("x", None, feat, None),
        check_vma=False,
    )
```
